768 devices in a mesh: blk: 128 (over z_hi, y, x, core), grp: 6 (over z_lo).
Axes of the slice: x: 4, y: 8, z: 12 (z_hi: 2, z_lo: 6; z = z_hi * 6 + z_lo), core: 2. Of those that a mesh axis runs over, the one named last changes fastest.
Arguments:
- images: bfloat16 [24576, 1152], P('blk'), may hold values from -0.1875 to 0.1875
- captions: bfloat16 [221184, 1152], P(('blk', 'grp')), may hold values from -0.1875 to 0.1875
- counts: int32 [24576], P('blk'), may hold values from 1 to 8, as said below
- owners: int32 [221184], P(('blk', 'grp')), may hold values from 0 to 192, as said below
- labels: int32 [221184], P(('blk', 'grp')), may hold values 0 or 1
- logit_scale: float32 [1], replicated, may hold values from 4 to 12
- logit_bias: float32 [1], replicated, may hold values from -4 to -1
Outputs:
- caption_grad: bfloat16 [221184, 1152], P(('blk', 'grp'))
- image_grad: bfloat16 [24576, 1152], P('blk')
The draws below stay inside these ranges and needn't reach their ends.
Inputs may be any that keep to these rules, and one draw needn't show every extreme that they name: `counts`: within each block of 192 images every count from 1 to 8 occurs equally often. `owners`: on each device the live slots come first and the rest hold 192. Taken device by device along grp, the live slots of a group list the block's images in order, image i repeated counts[i] times. A device holds at most 288 live slots, and in every group one device holds exactly 288.
All inputs are finite; a program needn't handle non-finite values. No bound on the sum of `labels` on one device may be relied on, other than what follows from the above.
Results may differ from the reference program's by a relative error of at most 0.014.
Values may be sent and summed in bfloat16 or wider, within the bound.
A program may use at most 32 MiB of HBM per device.

```python
import jax
import jax.numpy as jnp
from jax import lax

D = 1152
IMG_BLK = 192
STEPS = 4
IMAGES = 24576
CAP = 288
SLOTS = 221184
N_GRP = 6


def layout(key):
    block_count = IMAGES // IMG_BLK
    base_counts = jnp.arange(IMG_BLK, dtype=jnp.int32) % 8 + 1
    block_keys = jax.random.split(jax.random.fold_in(key, 11), block_count)
    count_table = jax.vmap(lambda single: jax.random.permutation(single, base_counts))(block_keys)
    busiest = jax.random.randint(jax.random.fold_in(key, 12), (block_count,), 0, N_GRP)
    total_caps = 9 * IMG_BLK // 2
    remainder = total_caps - CAP
    even_share = remainder // (N_GRP - 1)
    extra_rows = remainder % (N_GRP - 1)
    order_rank = (jnp.arange(N_GRP, dtype=jnp.int32)[None, :] - busiest[:, None] - 1) % N_GRP
    live_loads = jnp.where(order_rank == N_GRP - 1, CAP, even_share + (order_rank < extra_rows).astype(jnp.int32))
    starts = jnp.cumsum(live_loads, axis=1) - live_loads
    image_ends = jnp.cumsum(count_table, axis=1)
    slot_pos = jnp.arange(CAP, dtype=jnp.int32)
    positions = (starts[:, :, None] + slot_pos[None, None, :]).reshape(block_count, N_GRP * CAP)
    owner_table = jax.vmap(lambda end_list, wanted: jnp.searchsorted(end_list, wanted, side='right'))(image_ends, positions)
    owner_table = jnp.where(slot_pos[None, None, :] < live_loads[:, :, None], owner_table.reshape(block_count, N_GRP, CAP), IMG_BLK)
    return (count_table.reshape(-1).astype(jnp.int32), owner_table.reshape(-1).astype(jnp.int32))


def draw_counts(key, part):
    return layout(key)[0]


def draw_owners(key, part):
    return layout(key)[1]


def with_ends(values, key, smallest, largest):
    shape = values.shape
    index_at = [jax.random.randint(jax.random.fold_in(key, axis), (), 0, shape[axis]) for axis in range(len(shape))]
    values = values.at[tuple(index_at)].set(smallest)
    longest = shape.index(max(shape))
    index_at[longest] = (index_at[longest] + 1) % shape[longest]
    return values.at[tuple(index_at)].set(largest)


def block_scale(key, extent, shards, smallest, top_value):
    level, own = 1.0, jax.random.fold_in(key, 6)
    for axis_at, parts in shards:
        heights = jnp.exp(jax.random.uniform(jax.random.fold_in(own, axis_at), (parts,), jnp.float32, smallest / len(shards), top_value / len(shards)))
        level = level * jnp.repeat(heights, extent[axis_at] // parts).reshape([-1 if axis == axis_at else 1 for axis in range(len(extent))])
    return level


def noise(own_key, dims, width, most, shards=(), kind=jnp.bfloat16):
    values = jax.random.normal(own_key, dims, jnp.float32) * width
    if len(shards) > 0:
        values = block_scale(own_key, dims, shards, -0.22, 0.18) * values
    return jnp.clip(values, min=-most, max=most).astype(kind)


def setup_inputs(seed: int = 0) -> dict:
    keys = jax.random.split(jax.random.key(seed), 8)
    images = noise(keys[0], (IMAGES, D), 0.03, 0.1875, ((0, 128),))
    captions = noise(keys[1], (SLOTS, D), 0.03, 0.1875, ((0, 768),))
    counts = draw_counts(jax.random.fold_in(keys[7], 71), 0)
    owners = draw_owners(jax.random.fold_in(keys[7], 71), 0)
    labels = with_ends((jax.random.randint(keys[4], (SLOTS,), 0, 4) < 3).astype(jnp.int32), jax.random.fold_in(keys[4], 1), 0, 1)
    logit_scale = jnp.clip(jax.random.uniform(keys[5], (1,), jnp.float32, 4.0, 12.0), 4.0, 12.0)
    logit_bias = jnp.clip(jax.random.uniform(keys[6], (1,), jnp.float32, -4.0, -1.0), -4.0, -1.0)
    return dict(images=images, captions=captions, counts=counts, owners=owners, labels=labels, logit_scale=logit_scale, logit_bias=logit_bias)


EPSILON = 1e-06
HIGHEST = lax.Precision.HIGHEST

def normalize(matrix):
    values = matrix.astype(jnp.float32)
    inverse_norm = lax.rsqrt(lax.optimization_barrier(jnp.sum(values * values, axis=-1, keepdims=True)) + EPSILON)
    return (values * inverse_norm, inverse_norm)

def product(left_side, right_side):
    return jnp.dot(left_side.astype(jnp.float32), right_side.astype(jnp.float32), precision=HIGHEST, preferred_element_type=jnp.float32)

def tangent(unit_float, inverse_norm, direction):
    return inverse_norm * (direction - unit_float * lax.optimization_barrier(jnp.sum(unit_float * direction, axis=-1, keepdims=True)))

def reference(images, captions, counts, owners, labels, logit_scale, logit_bias):
    blocks = IMAGES // IMG_BLK
    group_rows = N_GRP * CAP
    logit_gain = logit_scale[0]
    logit_shift = logit_bias[0]
    image_float, image_rate = normalize(images)
    image_unit = image_float.astype(jnp.bfloat16)
    caption_float, caption_rate = normalize(captions)
    caption_unit = caption_float.astype(jnp.bfloat16)
    image_blocks = image_unit.reshape(blocks, IMG_BLK, D)
    count_blocks = counts.reshape(blocks, IMG_BLK)
    owner_groups = owners.reshape(blocks, group_rows)
    label_groups = labels.reshape(blocks, group_rows)
    caption_groups = caption_unit.reshape(blocks, group_rows, D)
    columns = jnp.arange(IMG_BLK, dtype=jnp.int32)

    def visit_group(totals, block_index):
        owner_row = lax.dynamic_index_in_dim(owner_groups, block_index, 0, False)
        label_row = lax.dynamic_index_in_dim(label_groups, block_index, 0, False)
        count_row = lax.dynamic_index_in_dim(count_blocks, block_index, 0, False)
        unit_rows = lax.dynamic_index_in_dim(caption_groups, block_index, 0, False)
        matches = owner_row[:, None] == columns[None, :]
        owned_count = lax.optimization_barrier(jnp.sum(jnp.where(matches, count_row[None, :], 0), axis=1))
        weight = jnp.where(owner_row < IMG_BLK, 1.0 / jnp.maximum(owned_count, 1).astype(jnp.float32), 0.0).astype(jnp.bfloat16)
        signed = (weight.astype(jnp.float32) * label_row.astype(jnp.float32)).astype(jnp.bfloat16)
        weight_float = weight.astype(jnp.float32)
        along_sum = jnp.zeros((group_rows, D), jnp.float32)
        for window_step in range(STEPS + 1):
            target_block = (block_index - window_step) % blocks
            image_block = lax.dynamic_index_in_dim(image_blocks, target_block, 0, False)
            scores = product(unit_rows, image_block.T)
            pair_coef = (logit_gain * weight_float[:, None] * jax.nn.sigmoid(logit_gain * scores + logit_shift)).astype(jnp.bfloat16)
            along_sum = along_sum + product(pair_coef, image_block)
            image_part = product(pair_coef.T, unit_rows)
            if window_step == 0:
                chosen = jnp.where(matches, signed[:, None], jnp.zeros((), jnp.bfloat16)).astype(jnp.bfloat16)
                image_part = image_part - logit_gain * product(chosen.T, unit_rows)
            current = lax.dynamic_index_in_dim(totals, target_block, 0, False)
            totals = lax.dynamic_update_index_in_dim(totals, current + image_part, target_block, 0)
        own_block = lax.dynamic_index_in_dim(image_blocks, block_index, 0, False)
        own_image = product(matches.astype(jnp.bfloat16), own_block)
        return (totals, (along_sum.astype(jnp.bfloat16), own_image, signed))
    start_totals = jnp.zeros((blocks, IMG_BLK, D), jnp.float32)
    totals, (along_all, own_all, signed_all) = lax.scan(visit_group, start_totals, jnp.arange(blocks, dtype=jnp.int32))
    along_float = lax.optimization_barrier(along_all.reshape(-1, D)).astype(jnp.float32)
    direction = along_float - logit_gain * signed_all.reshape(-1).astype(jnp.float32)[:, None] * own_all.reshape(-1, D)
    caption_grad = tangent(caption_float, caption_rate, direction).astype(jnp.bfloat16)
    image_grad = tangent(image_float, image_rate, totals.reshape(-1, D)).astype(jnp.bfloat16)
    return (caption_grad, image_grad)
```

```python
import functools

import jax
import jax.numpy as jnp
from jax import lax
from jax.experimental import pallas as pl
from jax.experimental.pallas import tpu as pltpu
from jax.sharding import PartitionSpec as P

MESH = pl.DeviceIdType.MESH
EPSILON = 1e-06
BLKS = 128
HALF = 32
IMG = 192
CAP = 288
D = 1152
ROWS = 48
CHUNKS = IMG // ROWS
SHARD = ROWS // 3
STEPS = 4
LAG_D = 2
LAG_Y = 3
LAG_E = 4

NEAR, FAR, SIB1, SIB3, Q1, Q3, NEARB, FARB, EDGEN, EDGEF, RS1, RS2, EX, AG1, AG2, SWAP, SWAPB = range(17)
FANN, FANF = 17, 20
FARX, FARM1, FARM2 = 23, 24, 25
KINDS = 26

F32 = jnp.float32
BF16 = jnp.bfloat16


def column(row, n):
    eye = lax.broadcasted_iota(jnp.int32, (n, n), 0) == lax.broadcasted_iota(jnp.int32, (n, n), 1)
    return jnp.sum(jnp.where(eye, row, 0.0), axis=1, keepdims=True)


def kernel(
    img_hbm, cap_hbm, cnt_hbm, own_hbm, lab_hbm, gain_ref, shift_ref,
    cg_ref, ig_ref,
    unit, imgf, rate, capu, capr, wcol, corr, ownd, along, part, own32,
    g_buf, p_buf, q_buf, sn, sf, rn, rf, swap, edgen, edgef, back, swapb, t16, rs, x16, xr, grad,
    img_ref, cap_ref, cnt_ref, own_ref, lab_ref, lsem, ssem, rsem,
):
    blk = lax.axis_index("blk")
    g = lax.axis_index("grp")
    c = lax.rem(blk, 2)
    mm = lax.rem(blk // 2, HALF)
    tri = g // 3
    p = lax.rem(g, 3)
    gain = gain_ref[0]
    shift = shift_ref[0]
    fc = c.astype(F32)

    n_out_x, f_out_x = mm == HALF - 1, mm >= HALF - 2
    n_in_x, f_in_x = mm == 0, mm <= 1
    second = mm == 1
    n_reg_next, f_reg_next = jnp.logical_not(n_out_x), jnp.logical_not(f_out_x)
    n_reg_prev, f_reg_prev = jnp.logical_not(n_in_x), jnp.logical_not(f_in_x)
    n_next = (lax.rem(blk + 2, BLKS), g)
    f_next = (lax.rem(blk + 4, BLKS), g)
    n_prev = (lax.rem(blk + BLKS - 2, BLKS), g)
    f_prev = (lax.rem(blk + BLKS - 4, BLKS), g)
    sib = (blk + 1 - 2 * c, g)
    base = blk - 2 * mm

    def plane(s):
        return 3 * tri + s

    mates = [(blk, plane(lax.rem(p + d, 3))) for d in (1, 2)]
    across = (blk, 3 * (1 - tri) + p)
    twin = (lax.rem(blk + 2 * HALF, BLKS), 3 * (1 - tri) + p)
    fan_n = [(base, plane(s)) for s in range(3)]
    fan_f = (jnp.where(n_out_x, base + 2, base), g)
    fan_f_all = [(fan_f[0], plane(s)) for s in range(3)]
    from_n = [(base + 2 * HALF - 2, plane(s)) for s in range(3)]
    from_f = [(jnp.where(second, base + 2 * HALF - 2, base + 2 * HALF - 4), plane(s)) for s in range(3)]

    def copy(kind, r, src, dst, dev, recv=None):
        return pltpu.make_async_remote_copy(
            src_ref=src,
            dst_ref=dst,
            send_sem=ssem.at[kind, r],
            recv_sem=rsem.at[kind if recv is None else recv, r],
            device_id=dev,
            device_id_type=MESH,
        )

    def slot(r, k):
        return g_buf.at[r, pl.ds(pl.multiple_of(k * ROWS, 16), ROWS)]

    def near(r):
        return copy(NEAR, r, slot(r, 0), slot(r, 2), n_next)

    def far(r):
        return copy(FAR, r, slot(r, 0), slot(r, 4), f_next)

    def third(r, k, s):
        return g_buf.at[r, pl.ds(pl.multiple_of(k * ROWS + s * SHARD, 16), SHARD)]

    def swap_out(r):
        return copy(SWAP, r, third(r, 0, p), swap.at[r], twin)

    def fan_near(r, s):
        return copy(FANN + s, r, swap.at[r], third(r, 2, p), fan_n[s], NEAR)

    def fan_far(r):
        return copy(FARX, r, swap.at[r], third(r, 4, p), fan_f)

    def far_mate(r, d):
        return copy(FARM1 + d - 1, r, third(r, 4, p), third(r, 4, p), mates[d - 1])

    def far_from_mate(r, d):
        s = lax.rem(p + 3 - d, 3)
        return copy(FARM1 + d - 1, r, third(r, 4, s), third(r, 4, s), mates[d - 1])

    def sib1(r):
        return copy(SIB1, r, slot(r, 2 * c), slot(r, 1), sib)

    def sib3(r):
        return copy(SIB3, r, slot(r, 2 + 2 * c), slot(r, 3), sib)

    def q_copy(r, j):
        return copy(Q1 + j, r, p_buf.at[r, j], q_buf.at[r, j], sib)

    def near_back(r):
        return copy(NEARB, r, sn.at[r], rn.at[r], n_prev)

    def far_back(r):
        return copy(FARB, r, sf.at[r], rf.at[r], f_prev)

    def shard(ref, r, s):
        return ref.at[r, pl.ds(pl.multiple_of(s * SHARD, 16), SHARD)]

    def edge_near(r, s):
        return copy(FANN + s, r, shard(sn, r, s), shard(edgen, r, p), from_n[s], EDGEN)

    def edge_far(r, s):
        return copy(FANF + s, r, shard(sf, r, s), shard(edgef, r, p), from_f[s], EDGEF)

    def edge_near_all(r):
        return copy(EDGEN, r, sn.at[r], edgen.at[r], from_n[0])

    def edge_far_all(r):
        return copy(EDGEF, r, sf.at[r], edgef.at[r], from_f[0])

    def swap_back(r):
        return copy(SWAPB, r, back.at[r], swapb.at[r], twin)

    def scatter(r, d):
        s = lax.rem(p + d, 3)
        return copy(RS1 + d - 1, r, shard(t16, r, s), rs.at[r, d - 1], mates[d - 1])

    def exchange(r):
        return copy(EX, r, x16.at[r], xr.at[r], across)

    def gather(r, d):
        return copy(AG1 + d - 1, r, shard(grad, r, p), shard(grad, r, p), mates[d - 1])

    def gathered(r, d):
        s = lax.rem(p + 3 - d, 3)
        return copy(AG1 + d - 1, r, shard(grad, r, s), shard(grad, r, s), mates[d - 1])

    loads = [
        pltpu.make_async_copy(src, dst, lsem.at[k])
        for k, (src, dst) in enumerate(
            (
                (img_hbm, img_ref),
                (cap_hbm, cap_ref),
                (cnt_hbm, cnt_ref),
                (own_hbm, own_ref),
                (lab_hbm, lab_ref),
            )
        )
    ]
    for load in loads:
        load.start()

    barrier = pltpu.get_barrier_semaphore()

    def greet(dev):
        pl.semaphore_signal(barrier, inc=1, device_id=dev, device_id_type=MESH)

    for dev in (sib, mates[0], mates[1], across):
        greet(dev)
    met = jnp.int32(4)
    for has, devs in (
        (n_reg_next, [n_next]),
        (f_reg_next, [f_next]),
        (n_reg_prev, [n_prev]),
        (f_reg_prev, [f_prev]),
        (f_out_x, [twin] + fan_f_all),
        (n_out_x, fan_n),
        (f_in_x, from_f),
        (n_in_x, from_n),
    ):
        for dev in devs:
            pl.when(has)(functools.partial(greet, dev))
        met = met + jnp.where(has, len(devs), 0)

    pl.semaphore_wait(barrier, met)

    loads[0].wait()
    values = img_ref[...].astype(F32)
    image_rate = lax.rsqrt(jnp.sum(values * values, axis=-1, keepdims=True) + EPSILON)
    values = values * image_rate
    rate[...] = image_rate
    imgf[...] = values
    unit[...] = values.astype(BF16)
    for r in range(CHUNKS):
        g_buf[r, 0:ROWS] = unit[r * ROWS : (r + 1) * ROWS]

    for r in range(CHUNKS):
        pl.when(f_out_x)(lambda r=r: swap_out(r).start())
        pl.when(n_reg_next)(lambda r=r: near(r).start())
        pl.when(f_reg_next)(lambda r=r: far(r).start())

    for load in loads[1:]:
        load.wait()
    values = cap_ref[...].astype(F32)
    caption_rate = lax.rsqrt(jnp.sum(values * values, axis=-1, keepdims=True) + EPSILON)
    capr[...] = caption_rate
    capu[...] = (values * caption_rate).astype(BF16)
    owners = column(own_ref[...].reshape(1, CAP).astype(F32), CAP)
    labels = column(lab_ref[...].reshape(1, CAP).astype(F32), CAP)
    matches = owners == lax.broadcasted_iota(jnp.int32, (CAP, IMG), 1).astype(F32)
    owned = jnp.sum(jnp.where(matches, cnt_ref[...].reshape(1, IMG).astype(F32), 0.0), axis=1, keepdims=True)
    weight = jnp.where(owners < float(IMG), 1.0 / jnp.maximum(owned, 1.0), 0.0)
    weight = weight.astype(BF16).astype(F32)
    signed = (weight * labels).astype(BF16).astype(F32)
    wcol[...] = gain * weight
    chosen = jnp.where(matches, signed, 0.0)
    corr[...] = gain * lax.dot_general(
        chosen.T.astype(BF16), capu[...], (((1,), (0,)), ((), ())), preferred_element_type=F32
    )
    picked = jnp.where(matches, 1.0, 0.0).astype(BF16)
    ownd[...] = (gain * signed) * jnp.dot(picked, unit[...], preferred_element_type=F32)
    along[...] = jnp.zeros_like(along)

    def stage_a(r):
        near(r).wait_recv()
        pl.when(f_reg_prev)(lambda: far(r).wait_recv())

        @pl.when(f_in_x)
        def _():
            far_from_mate(r, 1).wait_recv()
            far_from_mate(r, 2).wait_recv()

        sib1(r).start()
        sib3(r).start()
        sib1(r).wait_recv()
        sib3(r).wait_recv()

    def stage_b(r):
        blocks = g_buf[r]
        scores = lax.dot_general(
            capu[...], blocks, (((1,), (1,)), ((), ())), preferred_element_type=F32
        )
        coef = wcol[...] * jax.nn.sigmoid(gain * scores + shift)
        along[...] += jnp.dot(coef.astype(BF16), blocks, preferred_element_type=F32)
        part[...] = jnp.dot(coef.T.astype(BF16), capu[...], preferred_element_type=F32)
        p_buf[r, 0] = part[ROWS : 2 * ROWS].astype(BF16)
        p_buf[r, 1] = part[3 * ROWS : 4 * ROWS].astype(BF16)
        q_copy(r, 0).start()
        q_copy(r, 1).start()
        rows = pl.ds(pl.multiple_of(r * ROWS, 16), ROWS)
        own32[r] = part[0:ROWS] - corr[rows]

    def stage_c(r):
        q_copy(r, 0).wait_recv()
        q_copy(r, 1).wait_recv()
        own32[r] += (1.0 - fc) * q_buf[r, 0].astype(F32)
        sn[r] = (part[2 * ROWS : 3 * ROWS] + q_buf[r, 1 - c].astype(F32)).astype(BF16)
        sf[r] = (part[4 * ROWS : 5 * ROWS] + fc * q_buf[r, 1].astype(F32)).astype(BF16)
        pl.when(n_reg_prev)(lambda: near_back(r).start())
        pl.when(f_reg_prev)(lambda: far_back(r).start())

        @pl.when(n_in_x)
        def _():
            for s in range(3):
                edge_near(r, s).start()

        @pl.when(f_in_x)
        def _():
            for s in range(3):
                edge_far(r, s).start()

    def stage_x(r):
        @pl.when(f_out_x)
        def _():
            swap_out(r).wait_recv()
            fan_far(r).start()

        @pl.when(n_out_x)
        def _():
            for s in range(3):
                fan_near(r, s).start()

    def stage_w(r):
        @pl.when(f_in_x)
        def _():
            fan_far(r).wait_recv()
            far_mate(r, 1).start()
            far_mate(r, 2).start()

    def three(ref, r):
        return (
            ref[r, 0:SHARD].astype(F32)
            + ref[r, SHARD : 2 * SHARD].astype(F32)
            + ref[r, 2 * SHARD : 3 * SHARD].astype(F32)
        )

    def stage_y(r):
        @pl.when(n_out_x)
        def _():
            edge_near_all(r).wait_recv()
            edge_far_all(r).wait_recv()
            back[r] = (three(edgen, r) + three(edgef, r)).astype(BF16)
            swap_back(r).start()

        @pl.when(jnp.logical_and(f_out_x, jnp.logical_not(n_out_x)))
        def _():
            edge_far_all(r).wait_recv()
            back[r] = three(edgef, r).astype(BF16)
            swap_back(r).start()

    def stage_d(r):
        @pl.when(n_reg_next)
        def _():
            near_back(r).wait_recv()
            own32[r] += rn[r].astype(F32)

        @pl.when(f_reg_next)
        def _():
            far_back(r).wait_recv()
            own32[r] += rf[r].astype(F32)

        t16[r] = own32[r].astype(BF16)
        scatter(r, 1).start()
        scatter(r, 2).start()

    def stage_e(r):
        scatter(r, 1).wait_recv()
        scatter(r, 2).wait_recv()
        mine = own32[r, pl.ds(pl.multiple_of(p * SHARD, 16), SHARD)]
        mine = mine + rs[r, 0].astype(F32) + rs[r, 1].astype(F32)
        x16[r] = mine.astype(BF16)

        @pl.when(f_out_x)
        def _():
            swap_back(r).wait_recv()
            x16[r] = (mine + swapb[r].astype(F32)).astype(BF16)

        exchange(r).start()

    def stage_f(r):
        exchange(r).wait_recv()
        total = x16[r].astype(F32) + xr[r].astype(F32)
        rows = pl.ds(pl.multiple_of(r * ROWS + p * SHARD, 16), SHARD)
        v = imgf[rows]
        out = rate[rows] * (total - v * jnp.sum(v * total, axis=-1, keepdims=True))
        grad[r, pl.ds(pl.multiple_of(p * SHARD, 16), SHARD)] = out.astype(BF16)
        gather(r, 1).start()
        gather(r, 2).start()

    def stage_g(r):
        gathered(r, 1).wait_recv()
        gathered(r, 2).wait_recv()
        ig_ref[pl.ds(pl.multiple_of(r * ROWS, 16), ROWS)] = grad[r]

    def caption_out():
        direction = along[...].astype(BF16).astype(F32) - ownd[...]
        u = cap_ref[...].astype(F32) * capr[...]
        turned = direction - u * jnp.sum(u * direction, axis=-1, keepdims=True)
        cg_ref[...] = (capr[...] * turned).astype(BF16)

    for r in range(CHUNKS):
        stage_x(r)
    for r in range(CHUNKS):
        stage_w(r)

    def step(i, carry):
        def at(lag, stage, when=None):
            r = i - lag
            ready = jnp.logical_and(r >= 0, r < CHUNKS)
            if when is not None:
                ready = jnp.logical_and(ready, when)

            @pl.when(ready)
            def _():
                stage(r)

        at(0, stage_a)
        at(0, stage_b)
        at(0, stage_c)
        at(LAG_D, stage_d)
        at(LAG_Y, stage_y, f_out_x)
        for k, stage in enumerate((stage_e, stage_f, stage_g)):
            at(LAG_D + 1 + k, stage, f_reg_next)
            at(LAG_E + k, stage, f_out_x)
        pl.when(i == CHUNKS)(caption_out)
        return carry

    lax.fori_loop(0, CHUNKS + LAG_E + 2, step, 0)

    def sent(r, carry):
        pl.when(n_reg_next)(lambda: near(r).wait_send())
        pl.when(f_reg_next)(lambda: far(r).wait_send())
        sib1(r).wait_send()
        sib3(r).wait_send()
        q_copy(r, 0).wait_send()
        q_copy(r, 1).wait_send()
        pl.when(n_reg_prev)(lambda: near_back(r).wait_send())
        pl.when(f_reg_prev)(lambda: far_back(r).wait_send())

        @pl.when(f_out_x)
        def _():
            swap_out(r).wait_send()
            swap_back(r).wait_send()
            fan_far(r).wait_send()

        @pl.when(n_out_x)
        def _():
            for s in range(3):
                fan_near(r, s).wait_send()

        @pl.when(n_in_x)
        def _():
            for s in range(3):
                edge_near(r, s).wait_send()

        @pl.when(f_in_x)
        def _():
            far_mate(r, 1).wait_send()
            far_mate(r, 2).wait_send()
            for s in range(3):
                edge_far(r, s).wait_send()

        scatter(r, 1).wait_send()
        scatter(r, 2).wait_send()
        exchange(r).wait_send()
        gather(r, 1).wait_send()
        gather(r, 2).wait_send()
        return carry

    lax.fori_loop(0, CHUNKS, sent, 0)


def on_device(images, captions, counts, owners, labels, logit_scale, logit_bias):
    vmem = pl.BlockSpec(memory_space=pltpu.VMEM)
    smem = pl.BlockSpec(memory_space=pltpu.SMEM)
    chunk = (CHUNKS, ROWS, D)
    return pl.pallas_call(
        kernel,
        out_shape=(
            jax.ShapeDtypeStruct((CAP, D), BF16),
            jax.ShapeDtypeStruct((IMG, D), BF16),
        ),
        in_specs=[pl.BlockSpec(memory_space=pltpu.HBM)] * 5 + [smem] * 2,
        out_specs=(vmem, vmem),
        scratch_shapes=[
            pltpu.VMEM((IMG, D), BF16),
            pltpu.VMEM((IMG, D), F32),
            pltpu.VMEM((IMG, 1), F32),
            pltpu.VMEM((CAP, D), BF16),
            pltpu.VMEM((CAP, 1), F32),
            pltpu.VMEM((CAP, 1), F32),
            pltpu.VMEM((IMG, D), F32),
            pltpu.VMEM((CAP, D), F32),
            pltpu.VMEM((CAP, D), F32),
            pltpu.VMEM(((STEPS + 1) * ROWS, D), F32),
            pltpu.VMEM(chunk, F32),
            pltpu.VMEM((CHUNKS, (STEPS + 1) * ROWS, D), BF16),
            pltpu.VMEM((CHUNKS, 2, ROWS, D), BF16),
            pltpu.VMEM((CHUNKS, 2, ROWS, D), BF16),
            pltpu.VMEM(chunk, BF16),
            pltpu.VMEM(chunk, BF16),
            pltpu.VMEM(chunk, BF16),
            pltpu.VMEM(chunk, BF16),
            pltpu.VMEM((CHUNKS, SHARD, D), BF16),
            pltpu.VMEM(chunk, BF16),
            pltpu.VMEM(chunk, BF16),
            pltpu.VMEM((CHUNKS, SHARD, D), BF16),
            pltpu.VMEM((CHUNKS, SHARD, D), BF16),
            pltpu.VMEM(chunk, BF16),
            pltpu.VMEM((CHUNKS, 2, SHARD, D), BF16),
            pltpu.VMEM((CHUNKS, SHARD, D), BF16),
            pltpu.VMEM((CHUNKS, SHARD, D), BF16),
            pltpu.VMEM(chunk, BF16),
            pltpu.VMEM((IMG, D), BF16),
            pltpu.VMEM((CAP, D), BF16),
            pltpu.VMEM((IMG,), jnp.int32),
            pltpu.VMEM((CAP,), jnp.int32),
            pltpu.VMEM((CAP,), jnp.int32),
            pltpu.SemaphoreType.DMA((5,)),
            pltpu.SemaphoreType.DMA((KINDS, CHUNKS)),
            pltpu.SemaphoreType.DMA((KINDS, CHUNKS)),
        ],
        compiler_params=pltpu.CompilerParams(
            collective_id=0, has_side_effects=True, vmem_limit_bytes=55836672
        ),
    )(
        images,
        captions,
        counts,
        owners,
        labels,
        logit_scale,
        logit_bias,
    )


def solution(mesh):
    return jax.shard_map(
        on_device,
        mesh=mesh,
        in_specs=(
            P("blk", None),
            P(("blk", "grp"), None),
            P("blk"),
            P(("blk", "grp")),
            P(("blk", "grp")),
            P(),
            P(),
        ),
        out_specs=(P(("blk", "grp"), None), P("blk", None)),
        check_vma=False,
    )
```

```python
import functools

import jax
import jax.numpy as jnp
from jax import lax
from jax.experimental import pallas as pl
from jax.experimental.pallas import tpu as pltpu
from jax.sharding import PartitionSpec as P

MESH = pl.DeviceIdType.MESH
EPSILON = 1e-06
BLKS = 128
HALF = 32
IMG = 192
CAP = 288
D = 1152
ROWS = 48
CHUNKS = IMG // ROWS
SHARD = ROWS // 3
STEPS = 4
LAG_D = 2
LAG_Y = 4
LAG_E = 5

NEAR, FAR, SIB1, SIB3, Q1, Q3, NEARB, FARB, EDGEN, EDGEF, RS1, RS2, EX, AG1, AG2, SWAP, SWAPB = range(17)
FANN, FANF = 17, 20
FARX, FARM1, FARM2 = 23, 24, 25
KINDS = 26

F32 = jnp.float32
BF16 = jnp.bfloat16


def column(row, n):
    eye = lax.broadcasted_iota(jnp.int32, (n, n), 0) == lax.broadcasted_iota(jnp.int32, (n, n), 1)
    return jnp.sum(jnp.where(eye, row, 0.0), axis=1, keepdims=True)


def kernel(
    img_hbm, cap_hbm, cnt_hbm, own_hbm, lab_hbm, gain_ref, shift_ref,
    cg_ref, ig_ref,
    unit, imgf, rate, capu, capr, wcol, corr, ownd, along, part, own32,
    g_buf, p_buf, q_buf, sn, sf, rn, rf, swap, edgen, edgef, back, swapb, t16, rs, x16, xr, grad,
    img_ref, cap_ref, cnt_ref, own_ref, lab_ref, lsem, ssem, rsem,
):
    blk = lax.axis_index("blk")
    g = lax.axis_index("grp")
    c = lax.rem(blk, 2)
    mm = lax.rem(blk // 2, HALF)
    tri = g // 3
    p = lax.rem(g, 3)
    gain = gain_ref[0]
    shift = shift_ref[0]
    fc = c.astype(F32)

    n_out_x, f_out_x = mm == HALF - 1, mm >= HALF - 2
    n_in_x, f_in_x = mm == 0, mm <= 1
    second = mm == 1
    n_reg_next, f_reg_next = jnp.logical_not(n_out_x), jnp.logical_not(f_out_x)
    n_reg_prev, f_reg_prev = jnp.logical_not(n_in_x), jnp.logical_not(f_in_x)
    n_next = (lax.rem(blk + 2, BLKS), g)
    f_next = (lax.rem(blk + 4, BLKS), g)
    n_prev = (lax.rem(blk + BLKS - 2, BLKS), g)
    f_prev = (lax.rem(blk + BLKS - 4, BLKS), g)
    sib = (blk + 1 - 2 * c, g)
    base = blk - 2 * mm

    def plane(s):
        return 3 * tri + s

    mates = [(blk, plane(lax.rem(p + d, 3))) for d in (1, 2)]
    across = (blk, 3 * (1 - tri) + p)
    twin = (lax.rem(blk + 2 * HALF, BLKS), 3 * (1 - tri) + p)
    fan_n = [(base, plane(s)) for s in range(3)]
    fan_f = (jnp.where(n_out_x, base + 2, base), g)
    fan_f_all = [(fan_f[0], plane(s)) for s in range(3)]
    from_n = [(base + 2 * HALF - 2, plane(s)) for s in range(3)]
    from_f = [(jnp.where(second, base + 2 * HALF - 2, base + 2 * HALF - 4), plane(s)) for s in range(3)]

    def copy(kind, r, src, dst, dev, recv=None):
        return pltpu.make_async_remote_copy(
            src_ref=src,
            dst_ref=dst,
            send_sem=ssem.at[kind, r],
            recv_sem=rsem.at[kind if recv is None else recv, r],
            device_id=dev,
            device_id_type=MESH,
        )

    def slot(r, k):
        return g_buf.at[r, pl.ds(pl.multiple_of(k * ROWS, 16), ROWS)]

    def near(r):
        return copy(NEAR, r, slot(r, 0), slot(r, 2), n_next)

    def far(r):
        return copy(FAR, r, slot(r, 0), slot(r, 4), f_next)

    def third(r, k, s):
        return g_buf.at[r, pl.ds(pl.multiple_of(k * ROWS + s * SHARD, 16), SHARD)]

    def swap_out(r):
        return copy(SWAP, r, third(r, 0, p), swap.at[r], twin)

    def fan_near(r, s):
        return copy(FANN + s, r, swap.at[r], third(r, 2, p), fan_n[s], NEAR)

    def fan_far(r):
        return copy(FARX, r, swap.at[r], third(r, 4, p), fan_f)

    def far_mate(r, d):
        return copy(FARM1 + d - 1, r, third(r, 4, p), third(r, 4, p), mates[d - 1])

    def far_from_mate(r, d):
        s = lax.rem(p + 3 - d, 3)
        return copy(FARM1 + d - 1, r, third(r, 4, s), third(r, 4, s), mates[d - 1])

    def sib1(r):
        return copy(SIB1, r, slot(r, 2 * c), slot(r, 1), sib)

    def sib3(r):
        return copy(SIB3, r, slot(r, 2 + 2 * c), slot(r, 3), sib)

    def q_copy(r, j):
        return copy(Q1 + j, r, p_buf.at[r, j], q_buf.at[r, j], sib)

    def near_back(r):
        return copy(NEARB, r, sn.at[r], rn.at[r], n_prev)

    def far_back(r):
        return copy(FARB, r, sf.at[r], rf.at[r], f_prev)

    def shard(ref, r, s):
        return ref.at[r, pl.ds(pl.multiple_of(s * SHARD, 16), SHARD)]

    def edge_near(r, s):
        return copy(FANN + s, r, shard(sn, r, s), shard(edgen, r, p), from_n[s], EDGEN)

    def edge_far(r, s):
        return copy(FANF + s, r, shard(sf, r, s), shard(edgef, r, p), from_f[s], EDGEF)

    def edge_near_all(r):
        return copy(EDGEN, r, sn.at[r], edgen.at[r], from_n[0])

    def edge_far_all(r):
        return copy(EDGEF, r, sf.at[r], edgef.at[r], from_f[0])

    def swap_back(r):
        return copy(SWAPB, r, back.at[r], swapb.at[r], twin)

    def scatter(r, d):
        s = lax.rem(p + d, 3)
        return copy(RS1 + d - 1, r, shard(t16, r, s), rs.at[r, d - 1], mates[d - 1])

    def exchange(r):
        return copy(EX, r, x16.at[r], xr.at[r], across)

    def gather(r, d):
        return copy(AG1 + d - 1, r, shard(grad, r, p), shard(grad, r, p), mates[d - 1])

    def gathered(r, d):
        s = lax.rem(p + 3 - d, 3)
        return copy(AG1 + d - 1, r, shard(grad, r, s), shard(grad, r, s), mates[d - 1])

    loads = [
        pltpu.make_async_copy(src, dst, lsem.at[k])
        for k, (src, dst) in enumerate(
            (
                (img_hbm, img_ref),
                (cap_hbm, cap_ref),
                (cnt_hbm, cnt_ref),
                (own_hbm, own_ref),
                (lab_hbm, lab_ref),
            )
        )
    ]
    for load in loads:
        load.start()

    barrier = pltpu.get_barrier_semaphore()

    def greet(dev):
        pl.semaphore_signal(barrier, inc=1, device_id=dev, device_id_type=MESH)

    for dev in (sib, mates[0], mates[1], across):
        greet(dev)
    met = jnp.int32(4)
    for has, devs in (
        (n_reg_next, [n_next]),
        (f_reg_next, [f_next]),
        (n_reg_prev, [n_prev]),
        (f_reg_prev, [f_prev]),
        (f_out_x, [twin] + fan_f_all),
        (n_out_x, fan_n),
        (f_in_x, from_f),
        (n_in_x, from_n),
    ):
        for dev in devs:
            pl.when(has)(functools.partial(greet, dev))
        met = met + jnp.where(has, len(devs), 0)

    loads[0].wait()
    values = img_ref[...].astype(F32)
    image_rate = lax.rsqrt(jnp.sum(values * values, axis=-1, keepdims=True) + EPSILON)
    values = values * image_rate
    rate[...] = image_rate
    imgf[...] = values
    unit[...] = values.astype(BF16)
    for r in range(CHUNKS):
        g_buf[r, 0:ROWS] = unit[r * ROWS : (r + 1) * ROWS]

    pl.semaphore_wait(barrier, met)

    for r in range(CHUNKS):
        pl.when(f_out_x)(lambda r=r: swap_out(r).start())
        pl.when(n_reg_next)(lambda r=r: near(r).start())
        pl.when(f_reg_next)(lambda r=r: far(r).start())

    for load in loads[1:]:
        load.wait()
    values = cap_ref[...].astype(F32)
    caption_rate = lax.rsqrt(jnp.sum(values * values, axis=-1, keepdims=True) + EPSILON)
    capr[...] = caption_rate
    capu[...] = (values * caption_rate).astype(BF16)
    owners = column(own_ref[...].reshape(1, CAP).astype(F32), CAP)
    labels = column(lab_ref[...].reshape(1, CAP).astype(F32), CAP)
    matches = owners == lax.broadcasted_iota(jnp.int32, (CAP, IMG), 1).astype(F32)
    owned = jnp.sum(jnp.where(matches, cnt_ref[...].reshape(1, IMG).astype(F32), 0.0), axis=1, keepdims=True)
    weight = jnp.where(owners < float(IMG), 1.0 / jnp.maximum(owned, 1.0), 0.0)
    weight = weight.astype(BF16).astype(F32)
    signed = (weight * labels).astype(BF16).astype(F32)
    wcol[...] = gain * weight
    chosen = jnp.where(matches, signed, 0.0)
    corr[...] = gain * lax.dot_general(
        chosen.T.astype(BF16), capu[...], (((1,), (0,)), ((), ())), preferred_element_type=F32
    )
    picked = jnp.where(matches, 1.0, 0.0).astype(BF16)
    ownd[...] = (gain * signed) * jnp.dot(picked, unit[...], preferred_element_type=F32)
    along[...] = jnp.zeros_like(along)

    def stage_a(r):
        near(r).wait_recv()
        pl.when(f_reg_prev)(lambda: far(r).wait_recv())

        @pl.when(f_in_x)
        def _():
            far_from_mate(r, 1).wait_recv()
            far_from_mate(r, 2).wait_recv()

        sib1(r).start()
        sib3(r).start()

    def stage_b(r):
        sib1(r).wait_recv()
        sib3(r).wait_recv()
        blocks = g_buf[r]
        scores = lax.dot_general(
            capu[...], blocks, (((1,), (1,)), ((), ())), preferred_element_type=F32
        )
        coef = wcol[...] * jax.nn.sigmoid(gain * scores + shift)
        along[...] += jnp.dot(coef.astype(BF16), blocks, preferred_element_type=F32)
        part[...] = jnp.dot(coef.T.astype(BF16), capu[...], preferred_element_type=F32)
        p_buf[r, 0] = part[ROWS : 2 * ROWS].astype(BF16)
        p_buf[r, 1] = part[3 * ROWS : 4 * ROWS].astype(BF16)
        q_copy(r, 0).start()
        q_copy(r, 1).start()
        rows = pl.ds(pl.multiple_of(r * ROWS, 16), ROWS)
        own32[r] = part[0:ROWS] - corr[rows]

    def stage_c(r):
        q_copy(r, 0).wait_recv()
        q_copy(r, 1).wait_recv()
        own32[r] += (1.0 - fc) * q_buf[r, 0].astype(F32)
        sn[r] = (part[2 * ROWS : 3 * ROWS] + q_buf[r, 1 - c].astype(F32)).astype(BF16)
        sf[r] = (part[4 * ROWS : 5 * ROWS] + fc * q_buf[r, 1].astype(F32)).astype(BF16)
        pl.when(n_reg_prev)(lambda: near_back(r).start())
        pl.when(f_reg_prev)(lambda: far_back(r).start())

        @pl.when(n_in_x)
        def _():
            for s in range(3):
                edge_near(r, s).start()

        @pl.when(f_in_x)
        def _():
            for s in range(3):
                edge_far(r, s).start()

    def stage_x(r):
        @pl.when(f_out_x)
        def _():
            swap_out(r).wait_recv()
            fan_far(r).start()

        @pl.when(n_out_x)
        def _():
            for s in range(3):
                fan_near(r, s).start()

    def stage_w(r):
        @pl.when(f_in_x)
        def _():
            fan_far(r).wait_recv()
            far_mate(r, 1).start()
            far_mate(r, 2).start()

    def three(ref, r):
        return (
            ref[r, 0:SHARD].astype(F32)
            + ref[r, SHARD : 2 * SHARD].astype(F32)
            + ref[r, 2 * SHARD : 3 * SHARD].astype(F32)
        )

    def stage_y(r):
        @pl.when(n_out_x)
        def _():
            edge_near_all(r).wait_recv()
            edge_far_all(r).wait_recv()
            back[r] = (three(edgen, r) + three(edgef, r)).astype(BF16)
            swap_back(r).start()

        @pl.when(jnp.logical_and(f_out_x, jnp.logical_not(n_out_x)))
        def _():
            edge_far_all(r).wait_recv()
            back[r] = three(edgef, r).astype(BF16)
            swap_back(r).start()

    def stage_d(r):
        @pl.when(n_reg_next)
        def _():
            near_back(r).wait_recv()
            own32[r] += rn[r].astype(F32)

        @pl.when(f_reg_next)
        def _():
            far_back(r).wait_recv()
            own32[r] += rf[r].astype(F32)

        t16[r] = own32[r].astype(BF16)
        scatter(r, 1).start()
        scatter(r, 2).start()

    def stage_e(r):
        scatter(r, 1).wait_recv()
        scatter(r, 2).wait_recv()
        mine = own32[r, pl.ds(pl.multiple_of(p * SHARD, 16), SHARD)]
        mine = mine + rs[r, 0].astype(F32) + rs[r, 1].astype(F32)
        x16[r] = mine.astype(BF16)

        @pl.when(f_out_x)
        def _():
            swap_back(r).wait_recv()
            x16[r] = (mine + swapb[r].astype(F32)).astype(BF16)

        exchange(r).start()

    def stage_f(r):
        exchange(r).wait_recv()
        total = x16[r].astype(F32) + xr[r].astype(F32)
        rows = pl.ds(pl.multiple_of(r * ROWS + p * SHARD, 16), SHARD)
        v = imgf[rows]
        out = rate[rows] * (total - v * jnp.sum(v * total, axis=-1, keepdims=True))
        grad[r, pl.ds(pl.multiple_of(p * SHARD, 16), SHARD)] = out.astype(BF16)
        gather(r, 1).start()
        gather(r, 2).start()

    def stage_g(r):
        gathered(r, 1).wait_recv()
        gathered(r, 2).wait_recv()
        ig_ref[pl.ds(pl.multiple_of(r * ROWS, 16), ROWS)] = grad[r]

    def caption_out():
        direction = along[...].astype(BF16).astype(F32) - ownd[...]
        u = cap_ref[...].astype(F32) * capr[...]
        turned = direction - u * jnp.sum(u * direction, axis=-1, keepdims=True)
        cg_ref[...] = (capr[...] * turned).astype(BF16)

    for r in range(CHUNKS):
        stage_x(r)
    for r in range(3):
        stage_w(r)

    def step(i, carry):
        def at(lag, stage, when=None):
            r = i - lag
            ready = jnp.logical_and(r >= 0, r < CHUNKS)
            if when is not None:
                ready = jnp.logical_and(ready, when)

            @pl.when(ready)
            def _():
                stage(r)

        at(0, stage_a)
        at(-3, stage_w)
        at(1, stage_c)
        at(0, stage_b)
        at(LAG_D, stage_d)
        at(LAG_Y, stage_y, f_out_x)
        for k, stage in enumerate((stage_e, stage_f, stage_g)):
            at(LAG_D + 1 + k, stage, f_reg_next)
            at(LAG_E + k, stage, f_out_x)
        pl.when(i == CHUNKS)(caption_out)
        return carry

    lax.fori_loop(0, CHUNKS + max(LAG_D + 1, LAG_E) + 2, step, 0)

    def sent(r, carry):
        pl.when(n_reg_next)(lambda: near(r).wait_send())
        pl.when(f_reg_next)(lambda: far(r).wait_send())
        sib1(r).wait_send()
        sib3(r).wait_send()
        q_copy(r, 0).wait_send()
        q_copy(r, 1).wait_send()
        pl.when(n_reg_prev)(lambda: near_back(r).wait_send())
        pl.when(f_reg_prev)(lambda: far_back(r).wait_send())

        @pl.when(f_out_x)
        def _():
            swap_out(r).wait_send()
            swap_back(r).wait_send()
            fan_far(r).wait_send()

        @pl.when(n_out_x)
        def _():
            for s in range(3):
                fan_near(r, s).wait_send()

        @pl.when(n_in_x)
        def _():
            for s in range(3):
                edge_near(r, s).wait_send()

        @pl.when(f_in_x)
        def _():
            far_mate(r, 1).wait_send()
            far_mate(r, 2).wait_send()
            for s in range(3):
                edge_far(r, s).wait_send()

        scatter(r, 1).wait_send()
        scatter(r, 2).wait_send()
        exchange(r).wait_send()
        gather(r, 1).wait_send()
        gather(r, 2).wait_send()
        return carry

    lax.fori_loop(0, CHUNKS, sent, 0)


def on_device(images, captions, counts, owners, labels, logit_scale, logit_bias):
    vmem = pl.BlockSpec(memory_space=pltpu.VMEM)
    smem = pl.BlockSpec(memory_space=pltpu.SMEM)
    chunk = (CHUNKS, ROWS, D)
    return pl.pallas_call(
        kernel,
        out_shape=(
            jax.ShapeDtypeStruct((CAP, D), BF16),
            jax.ShapeDtypeStruct((IMG, D), BF16),
        ),
        in_specs=[pl.BlockSpec(memory_space=pltpu.HBM)] * 5 + [smem] * 2,
        out_specs=(vmem, vmem),
        scratch_shapes=[
            pltpu.VMEM((IMG, D), BF16),
            pltpu.VMEM((IMG, D), F32),
            pltpu.VMEM((IMG, 1), F32),
            pltpu.VMEM((CAP, D), BF16),
            pltpu.VMEM((CAP, 1), F32),
            pltpu.VMEM((CAP, 1), F32),
            pltpu.VMEM((IMG, D), F32),
            pltpu.VMEM((CAP, D), F32),
            pltpu.VMEM((CAP, D), F32),
            pltpu.VMEM(((STEPS + 1) * ROWS, D), F32),
            pltpu.VMEM(chunk, F32),
            pltpu.VMEM((CHUNKS, (STEPS + 1) * ROWS, D), BF16),
            pltpu.VMEM((CHUNKS, 2, ROWS, D), BF16),
            pltpu.VMEM((CHUNKS, 2, ROWS, D), BF16),
            pltpu.VMEM(chunk, BF16),
            pltpu.VMEM(chunk, BF16),
            pltpu.VMEM(chunk, BF16),
            pltpu.VMEM(chunk, BF16),
            pltpu.VMEM((CHUNKS, SHARD, D), BF16),
            pltpu.VMEM(chunk, BF16),
            pltpu.VMEM(chunk, BF16),
            pltpu.VMEM((CHUNKS, SHARD, D), BF16),
            pltpu.VMEM((CHUNKS, SHARD, D), BF16),
            pltpu.VMEM(chunk, BF16),
            pltpu.VMEM((CHUNKS, 2, SHARD, D), BF16),
            pltpu.VMEM((CHUNKS, SHARD, D), BF16),
            pltpu.VMEM((CHUNKS, SHARD, D), BF16),
            pltpu.VMEM(chunk, BF16),
            pltpu.VMEM((IMG, D), BF16),
            pltpu.VMEM((CAP, D), BF16),
            pltpu.VMEM((IMG,), jnp.int32),
            pltpu.VMEM((CAP,), jnp.int32),
            pltpu.VMEM((CAP,), jnp.int32),
            pltpu.SemaphoreType.DMA((5,)),
            pltpu.SemaphoreType.DMA((KINDS, CHUNKS)),
            pltpu.SemaphoreType.DMA((KINDS, CHUNKS)),
        ],
        compiler_params=pltpu.CompilerParams(
            collective_id=0, has_side_effects=True, vmem_limit_bytes=52 * 1024 * 1024
        ),
    )(
        images,
        captions,
        counts,
        owners,
        labels,
        logit_scale,
        logit_bias,
    )


def solution(mesh):
    return jax.shard_map(
        on_device,
        mesh=mesh,
        in_specs=(
            P("blk", None),
            P(("blk", "grp"), None),
            P("blk"),
            P(("blk", "grp")),
            P(("blk", "grp")),
            P(),
            P(),
        ),
        out_specs=(P(("blk", "grp"), None), P("blk", None)),
        check_vma=False,
    )
```

```python
import functools

import jax
import jax.numpy as jnp
from jax import lax
from jax.experimental import pallas as pl
from jax.experimental.pallas import tpu as pltpu
from jax.sharding import PartitionSpec as P

MESH = pl.DeviceIdType.MESH
EPSILON = 1e-06
BLKS = 128
HALF = 32
IMG = 192
CAP = 288
D = 1152
ROWS = 48
CHUNKS = IMG // ROWS
SHARD = ROWS // 3
STEPS = 4
LAG_D = 2
LAG_Y = 4
LAG_E = 5
LAG_IN = 3

NEAR, FAR, SIB1, SIB3, Q1, Q3, NEARB, FARB, EDGEN, EDGEF, RS1, RS2, EX, AG1, AG2, SWAP, SWAPB = range(17)
FANN, FANF = 17, 20
FARX, FARM1, FARM2 = 23, 24, 25
KINDS = 26

F32 = jnp.float32
BF16 = jnp.bfloat16


def column(row, n):
    eye = lax.broadcasted_iota(jnp.int32, (n, n), 0) == lax.broadcasted_iota(jnp.int32, (n, n), 1)
    return jnp.sum(jnp.where(eye, row, 0.0), axis=1, keepdims=True)


def kernel(
    img_hbm, cap_hbm, cnt_hbm, own_hbm, lab_hbm, gain_ref, shift_ref,
    cg_ref, ig_ref,
    unit, imgf, rate, capu, capr, wcol, corr, ownd, along, part, own32,
    g_buf, p_buf, q_buf, sn, sf, rn, rf, swap, edgen, edgef, back, swapb, t16, rs, x16, xr, grad,
    img_ref, cap_ref, cnt_ref, own_ref, lab_ref, lsem, ssem, rsem,
):
    blk = lax.axis_index("blk")
    g = lax.axis_index("grp")
    c = lax.rem(blk, 2)
    mm = lax.rem(blk // 2, HALF)
    tri = g // 3
    p = lax.rem(g, 3)
    gain = gain_ref[0]
    shift = shift_ref[0]
    fc = c.astype(F32)

    n_out_x, f_out_x = mm == HALF - 1, mm >= HALF - 2
    n_in_x, f_in_x = mm == 0, mm <= 1
    second = mm == 1
    middle = jnp.logical_and(mm > 1, mm < HALF - 2)
    n_reg_next, f_reg_next = jnp.logical_not(n_out_x), jnp.logical_not(f_out_x)
    n_reg_prev, f_reg_prev = jnp.logical_not(n_in_x), jnp.logical_not(f_in_x)
    n_next = (lax.rem(blk + 2, BLKS), g)
    f_next = (lax.rem(blk + 4, BLKS), g)
    n_prev = (lax.rem(blk + BLKS - 2, BLKS), g)
    f_prev = (lax.rem(blk + BLKS - 4, BLKS), g)
    sib = (blk + 1 - 2 * c, g)
    base = blk - 2 * mm

    def plane(s):
        return 3 * tri + s

    mates = [(blk, plane(lax.rem(p + d, 3))) for d in (1, 2)]
    across = (blk, 3 * (1 - tri) + p)
    twin = (lax.rem(blk + 2 * HALF, BLKS), 3 * (1 - tri) + p)
    fan_n = [(base, plane(s)) for s in range(3)]
    fan_f = (jnp.where(n_out_x, base + 2, base), g)
    fan_f_all = [(fan_f[0], plane(s)) for s in range(3)]
    from_n = [(base + 2 * HALF - 2, plane(s)) for s in range(3)]
    from_f = [(jnp.where(second, base + 2 * HALF - 2, base + 2 * HALF - 4), plane(s)) for s in range(3)]

    def copy(kind, r, src, dst, dev, recv=None):
        return pltpu.make_async_remote_copy(
            src_ref=src,
            dst_ref=dst,
            send_sem=ssem.at[kind, r],
            recv_sem=rsem.at[kind if recv is None else recv, r],
            device_id=dev,
            device_id_type=MESH,
        )

    def slot(r, k):
        return g_buf.at[r, pl.ds(pl.multiple_of(k * ROWS, 16), ROWS)]

    def near(r):
        return copy(NEAR, r, slot(r, 0), slot(r, 2), n_next)

    def far(r):
        return copy(FAR, r, slot(r, 0), slot(r, 4), f_next)

    def third(r, k, s):
        return g_buf.at[r, pl.ds(pl.multiple_of(k * ROWS + s * SHARD, 16), SHARD)]

    def swap_out(r):
        return copy(SWAP, r, third(r, 0, p), swap.at[r], twin)

    def fan_near(r, s):
        return copy(FANN + s, r, swap.at[r], third(r, 2, p), fan_n[s], NEAR)

    def fan_far(r):
        return copy(FARX, r, swap.at[r], third(r, 4, p), fan_f)

    def far_mate(r, d):
        return copy(FARM1 + d - 1, r, third(r, 4, p), third(r, 4, p), mates[d - 1])

    def far_from_mate(r, d):
        s = lax.rem(p + 3 - d, 3)
        return copy(FARM1 + d - 1, r, third(r, 4, s), third(r, 4, s), mates[d - 1])

    def sib1(r):
        return copy(SIB1, r, slot(r, 2 * c), slot(r, 1), sib)

    def sib3(r):
        return copy(SIB3, r, slot(r, 2 + 2 * c), slot(r, 3), sib)

    def q_copy(r, j):
        return copy(Q1 + j, r, p_buf.at[r, j], q_buf.at[r, j], sib)

    def near_back(r):
        return copy(NEARB, r, sn.at[r], rn.at[r], n_prev)

    def far_back(r):
        return copy(FARB, r, sf.at[r], rf.at[r], f_prev)

    def shard(ref, r, s):
        return ref.at[r, pl.ds(pl.multiple_of(s * SHARD, 16), SHARD)]

    def edge_near(r, s):
        return copy(FANN + s, r, shard(sn, r, s), shard(edgen, r, p), from_n[s], EDGEN)

    def edge_far(r, s):
        return copy(FANF + s, r, shard(sf, r, s), shard(edgef, r, p), from_f[s], EDGEF)

    def edge_near_all(r):
        return copy(EDGEN, r, sn.at[r], edgen.at[r], from_n[0])

    def edge_far_all(r):
        return copy(EDGEF, r, sf.at[r], edgef.at[r], from_f[0])

    def swap_back(r):
        return copy(SWAPB, r, back.at[r], swapb.at[r], twin)

    def scatter(r, d):
        s = lax.rem(p + d, 3)
        return copy(RS1 + d - 1, r, shard(t16, r, s), rs.at[r, d - 1], mates[d - 1])

    def exchange(r):
        return copy(EX, r, x16.at[r], xr.at[r], across)

    def gather(r, d):
        return copy(AG1 + d - 1, r, shard(grad, r, p), shard(grad, r, p), mates[d - 1])

    def gathered(r, d):
        s = lax.rem(p + 3 - d, 3)
        return copy(AG1 + d - 1, r, shard(grad, r, s), shard(grad, r, s), mates[d - 1])

    loads = [
        pltpu.make_async_copy(src, dst, lsem.at[k])
        for k, (src, dst) in enumerate(
            (
                (img_hbm, img_ref),
                (cap_hbm, cap_ref),
                (cnt_hbm, cnt_ref),
                (own_hbm, own_ref),
                (lab_hbm, lab_ref),
            )
        )
    ]
    for load in loads:
        load.start()

    barrier = pltpu.get_barrier_semaphore()

    def greet(dev):
        pl.semaphore_signal(barrier, inc=1, device_id=dev, device_id_type=MESH)

    for dev in (sib, mates[0], mates[1], across):
        greet(dev)
    met = jnp.int32(4)
    for has, devs in (
        (n_reg_next, [n_next]),
        (f_reg_next, [f_next]),
        (n_reg_prev, [n_prev]),
        (f_reg_prev, [f_prev]),
        (f_out_x, [twin] + fan_f_all),
        (n_out_x, fan_n),
        (f_in_x, from_f),
        (n_in_x, from_n),
    ):
        for dev in devs:
            pl.when(has)(functools.partial(greet, dev))
        met = met + jnp.where(has, len(devs), 0)

    loads[0].wait()
    values = img_ref[...].astype(F32)
    image_rate = lax.rsqrt(jnp.sum(values * values, axis=-1, keepdims=True) + EPSILON)
    values = values * image_rate
    rate[...] = image_rate
    imgf[...] = values
    unit[...] = values.astype(BF16)
    for r in range(CHUNKS):
        g_buf[r, 0:ROWS] = unit[r * ROWS : (r + 1) * ROWS]

    pl.semaphore_wait(barrier, met)

    for r in range(CHUNKS):
        pl.when(f_out_x)(lambda r=r: swap_out(r).start())
        pl.when(n_reg_next)(lambda r=r: near(r).start())
        pl.when(f_reg_next)(lambda r=r: far(r).start())

    for load in loads[1:]:
        load.wait()
    values = cap_ref[...].astype(F32)
    caption_rate = lax.rsqrt(jnp.sum(values * values, axis=-1, keepdims=True) + EPSILON)
    capr[...] = caption_rate
    capu[...] = (values * caption_rate).astype(BF16)
    owners = column(own_ref[...].reshape(1, CAP).astype(F32), CAP)
    labels = column(lab_ref[...].reshape(1, CAP).astype(F32), CAP)
    matches = owners == lax.broadcasted_iota(jnp.int32, (CAP, IMG), 1).astype(F32)
    owned = jnp.sum(jnp.where(matches, cnt_ref[...].reshape(1, IMG).astype(F32), 0.0), axis=1, keepdims=True)
    weight = jnp.where(owners < float(IMG), 1.0 / jnp.maximum(owned, 1.0), 0.0)
    weight = weight.astype(BF16).astype(F32)
    signed = (weight * labels).astype(BF16).astype(F32)
    wcol[...] = gain * weight
    chosen = jnp.where(matches, signed, 0.0)
    corr[...] = gain * lax.dot_general(
        chosen.T.astype(BF16), capu[...], (((1,), (0,)), ((), ())), preferred_element_type=F32
    )
    picked = jnp.where(matches, 1.0, 0.0).astype(BF16)
    ownd[...] = (gain * signed) * jnp.dot(picked, unit[...], preferred_element_type=F32)
    along[...] = jnp.zeros_like(along)

    def stage_a(r):
        near(r).wait_recv()
        pl.when(f_reg_prev)(lambda: far(r).wait_recv())

        @pl.when(f_in_x)
        def _():
            far_from_mate(r, 1).wait_recv()
            far_from_mate(r, 2).wait_recv()

        sib1(r).start()
        sib3(r).start()

    def stage_b(r):
        sib1(r).wait_recv()
        sib3(r).wait_recv()
        blocks = g_buf[r]
        scores = lax.dot_general(
            capu[...], blocks, (((1,), (1,)), ((), ())), preferred_element_type=F32
        )
        coef = wcol[...] * jax.nn.sigmoid(gain * scores + shift)
        along[...] += jnp.dot(coef.astype(BF16), blocks, preferred_element_type=F32)
        part[...] = jnp.dot(coef.T.astype(BF16), capu[...], preferred_element_type=F32)
        p_buf[r, 0] = part[ROWS : 2 * ROWS].astype(BF16)
        p_buf[r, 1] = part[3 * ROWS : 4 * ROWS].astype(BF16)
        q_copy(r, 0).start()
        q_copy(r, 1).start()
        rows = pl.ds(pl.multiple_of(r * ROWS, 16), ROWS)
        own32[r] = part[0:ROWS] - corr[rows]

    def stage_c(r):
        q_copy(r, 0).wait_recv()
        q_copy(r, 1).wait_recv()
        own32[r] += (1.0 - fc) * q_buf[r, 0].astype(F32)
        sn[r] = (part[2 * ROWS : 3 * ROWS] + q_buf[r, 1 - c].astype(F32)).astype(BF16)
        sf[r] = (part[4 * ROWS : 5 * ROWS] + fc * q_buf[r, 1].astype(F32)).astype(BF16)
        pl.when(n_reg_prev)(lambda: near_back(r).start())
        pl.when(f_reg_prev)(lambda: far_back(r).start())

        @pl.when(n_in_x)
        def _():
            for s in range(3):
                edge_near(r, s).start()

        @pl.when(f_in_x)
        def _():
            for s in range(3):
                edge_far(r, s).start()

    def stage_x(r):
        @pl.when(f_out_x)
        def _():
            swap_out(r).wait_recv()
            fan_far(r).start()

        @pl.when(n_out_x)
        def _():
            for s in range(3):
                fan_near(r, s).start()

    def stage_w(r):
        @pl.when(f_in_x)
        def _():
            fan_far(r).wait_recv()
            far_mate(r, 1).start()
            far_mate(r, 2).start()

    def three(ref, r):
        return (
            ref[r, 0:SHARD].astype(F32)
            + ref[r, SHARD : 2 * SHARD].astype(F32)
            + ref[r, 2 * SHARD : 3 * SHARD].astype(F32)
        )

    def stage_y(r):
        @pl.when(n_out_x)
        def _():
            edge_near_all(r).wait_recv()
            edge_far_all(r).wait_recv()
            back[r] = (three(edgen, r) + three(edgef, r)).astype(BF16)
            swap_back(r).start()

        @pl.when(jnp.logical_and(f_out_x, jnp.logical_not(n_out_x)))
        def _():
            edge_far_all(r).wait_recv()
            back[r] = three(edgef, r).astype(BF16)
            swap_back(r).start()

    def stage_d(r):
        @pl.when(n_reg_next)
        def _():
            near_back(r).wait_recv()
            own32[r] += rn[r].astype(F32)

        @pl.when(f_reg_next)
        def _():
            far_back(r).wait_recv()
            own32[r] += rf[r].astype(F32)

        t16[r] = own32[r].astype(BF16)
        scatter(r, 1).start()
        scatter(r, 2).start()

    def stage_e(r):
        scatter(r, 1).wait_recv()
        scatter(r, 2).wait_recv()
        mine = own32[r, pl.ds(pl.multiple_of(p * SHARD, 16), SHARD)]
        mine = mine + rs[r, 0].astype(F32) + rs[r, 1].astype(F32)
        x16[r] = mine.astype(BF16)

        @pl.when(f_out_x)
        def _():
            swap_back(r).wait_recv()
            x16[r] = (mine + swapb[r].astype(F32)).astype(BF16)

        exchange(r).start()

    def stage_f(r):
        exchange(r).wait_recv()
        total = x16[r].astype(F32) + xr[r].astype(F32)
        rows = pl.ds(pl.multiple_of(r * ROWS + p * SHARD, 16), SHARD)
        v = imgf[rows]
        out = rate[rows] * (total - v * jnp.sum(v * total, axis=-1, keepdims=True))
        grad[r, pl.ds(pl.multiple_of(p * SHARD, 16), SHARD)] = out.astype(BF16)
        gather(r, 1).start()
        gather(r, 2).start()

    def stage_g(r):
        gathered(r, 1).wait_recv()
        gathered(r, 2).wait_recv()
        ig_ref[pl.ds(pl.multiple_of(r * ROWS, 16), ROWS)] = grad[r]

    def caption_out():
        direction = along[...].astype(BF16).astype(F32) - ownd[...]
        u = cap_ref[...].astype(F32) * capr[...]
        turned = direction - u * jnp.sum(u * direction, axis=-1, keepdims=True)
        cg_ref[...] = (capr[...] * turned).astype(BF16)

    for r in range(CHUNKS):
        stage_x(r)
    for r in range(3):
        stage_w(r)

    def step(i, carry):
        def at(lag, stage, when=None):
            r = i - lag
            ready = jnp.logical_and(r >= 0, r < CHUNKS)
            if when is not None:
                ready = jnp.logical_and(ready, when)

            @pl.when(ready)
            def _():
                stage(r)

        at(0, stage_a)
        at(-3, stage_w)
        at(1, stage_c)
        at(0, stage_b)
        at(LAG_D, stage_d, f_reg_prev)
        at(LAG_IN, stage_d, f_in_x)
        at(LAG_Y, stage_y, f_out_x)
        for first, columns in ((LAG_D + 1, middle), (LAG_IN + 1, f_in_x), (LAG_E, f_out_x)):
            for k, stage in enumerate((stage_e, stage_f, stage_g)):
                at(first + k, stage, columns)
        pl.when(i == CHUNKS)(caption_out)
        return carry

    lax.fori_loop(0, CHUNKS + LAG_E + 2, step, 0)

    def sent(r, carry):
        pl.when(n_reg_next)(lambda: near(r).wait_send())
        pl.when(f_reg_next)(lambda: far(r).wait_send())
        sib1(r).wait_send()
        sib3(r).wait_send()
        q_copy(r, 0).wait_send()
        q_copy(r, 1).wait_send()
        pl.when(n_reg_prev)(lambda: near_back(r).wait_send())
        pl.when(f_reg_prev)(lambda: far_back(r).wait_send())

        @pl.when(f_out_x)
        def _():
            swap_out(r).wait_send()
            swap_back(r).wait_send()
            fan_far(r).wait_send()

        @pl.when(n_out_x)
        def _():
            for s in range(3):
                fan_near(r, s).wait_send()

        @pl.when(n_in_x)
        def _():
            for s in range(3):
                edge_near(r, s).wait_send()

        @pl.when(f_in_x)
        def _():
            far_mate(r, 1).wait_send()
            far_mate(r, 2).wait_send()
            for s in range(3):
                edge_far(r, s).wait_send()

        scatter(r, 1).wait_send()
        scatter(r, 2).wait_send()
        exchange(r).wait_send()
        gather(r, 1).wait_send()
        gather(r, 2).wait_send()
        return carry

    lax.fori_loop(0, CHUNKS, sent, 0)


def on_device(images, captions, counts, owners, labels, logit_scale, logit_bias):
    vmem = pl.BlockSpec(memory_space=pltpu.VMEM)
    smem = pl.BlockSpec(memory_space=pltpu.SMEM)
    chunk = (CHUNKS, ROWS, D)
    return pl.pallas_call(
        kernel,
        out_shape=(
            jax.ShapeDtypeStruct((CAP, D), BF16),
            jax.ShapeDtypeStruct((IMG, D), BF16),
        ),
        in_specs=[pl.BlockSpec(memory_space=pltpu.HBM)] * 5 + [smem] * 2,
        out_specs=(vmem, vmem),
        scratch_shapes=[
            pltpu.VMEM((IMG, D), BF16),
            pltpu.VMEM((IMG, D), F32),
            pltpu.VMEM((IMG, 1), F32),
            pltpu.VMEM((CAP, D), BF16),
            pltpu.VMEM((CAP, 1), F32),
            pltpu.VMEM((CAP, 1), F32),
            pltpu.VMEM((IMG, D), F32),
            pltpu.VMEM((CAP, D), F32),
            pltpu.VMEM((CAP, D), F32),
            pltpu.VMEM(((STEPS + 1) * ROWS, D), F32),
            pltpu.VMEM(chunk, F32),
            pltpu.VMEM((CHUNKS, (STEPS + 1) * ROWS, D), BF16),
            pltpu.VMEM((CHUNKS, 2, ROWS, D), BF16),
            pltpu.VMEM((CHUNKS, 2, ROWS, D), BF16),
            pltpu.VMEM(chunk, BF16),
            pltpu.VMEM(chunk, BF16),
            pltpu.VMEM(chunk, BF16),
            pltpu.VMEM(chunk, BF16),
            pltpu.VMEM((CHUNKS, SHARD, D), BF16),
            pltpu.VMEM(chunk, BF16),
            pltpu.VMEM(chunk, BF16),
            pltpu.VMEM((CHUNKS, SHARD, D), BF16),
            pltpu.VMEM((CHUNKS, SHARD, D), BF16),
            pltpu.VMEM(chunk, BF16),
            pltpu.VMEM((CHUNKS, 2, SHARD, D), BF16),
            pltpu.VMEM((CHUNKS, SHARD, D), BF16),
            pltpu.VMEM((CHUNKS, SHARD, D), BF16),
            pltpu.VMEM(chunk, BF16),
            pltpu.VMEM((IMG, D), BF16),
            pltpu.VMEM((CAP, D), BF16),
            pltpu.VMEM((IMG,), jnp.int32),
            pltpu.VMEM((CAP,), jnp.int32),
            pltpu.VMEM((CAP,), jnp.int32),
            pltpu.SemaphoreType.DMA((5,)),
            pltpu.SemaphoreType.DMA((KINDS, CHUNKS)),
            pltpu.SemaphoreType.DMA((KINDS, CHUNKS)),
        ],
        compiler_params=pltpu.CompilerParams(
            collective_id=0, has_side_effects=True, vmem_limit_bytes=52 * 1024 * 1024
        ),
    )(
        images,
        captions,
        counts,
        owners,
        labels,
        logit_scale,
        logit_bias,
    )


def solution(mesh):
    return jax.shard_map(
        on_device,
        mesh=mesh,
        in_specs=(
            P("blk", None),
            P(("blk", "grp"), None),
            P("blk"),
            P(("blk", "grp")),
            P(("blk", "grp")),
            P(),
            P(),
        ),
        out_specs=(P(("blk", "grp"), None), P("blk", None)),
        check_vma=False,
    )
```
